32 devices in a mesh: groups: 2 (over y), row: 4 (over z), col: 4 (over x, core).
Axes of the slice: x: 2, y: 2, z: 4, core: 2. Of those that a mesh axis runs over, the one named last changes fastest.
Arguments:
- positions: float32 [4096, 3, 128], P(('groups', 'row', 'col')), parts along dimension 0, may hold values from -6 to 6
- normals: float32 [4096, 3, 128], P(('groups', 'row', 'col')), parts along dimension 0, may hold values from -6 to 6
- curvature: float32 [4096, 128], P(('groups', 'row', 'col')), parts along dimension 0, may hold values from 0.5 to 3
- pair_targets: int32 [32, 512], P(('groups', 'row', 'col')), parts along dimension 0, may hold values from 0 to 511, as said below
- pair_sources: int32 [32, 512], P(('groups', 'row', 'col')), parts along dimension 0, may hold values from 0 to 511
- pair_count: int32 [32], P(('groups', 'row', 'col')), parts along dimension 0, may hold values from 64 to 512, as said below
- node_counts: int32 [512, 8], P('groups'), parts along dimension 0, may hold values from 1 to 128, 642 in all within a row
- drop_clusters: int32 [512, 8], P('groups'), parts along dimension 0, may hold values from 0 to 2047, as said below
- drop_owner: int32 [512], P('groups'), parts along dimension 0, may hold values from 0 to 15, as said below
Outputs:
- drop_velocity: float32 [4096, 3, 128], P(('groups', 'row', 'col')), parts along dimension 0
The draws below stay inside these ranges and needn't reach their ends.
There are 2 independent parts, one for each index of `groups`. The reference program is written for one: setup_inputs(seed, part) draws one part's arguments, and reference() takes and returns one part's arrays. A program takes and returns all parts, laid end to end along the dimension named above; each array names one. Nothing has to cross between parts.
Inputs may be any that keep to these rules, and one draw needn't show every extreme that they name: `drop_clusters`: every cluster of 0 to 2047 appears exactly once. Of the 128 clusters of one device, at most 16 belong to drops of any one owner, and this many is reached. `drop_owner`: every device owns exactly 16 drops. `pair_count`: the largest count is reached on some device; list entries past a device's count are not pairs. In each device's list, at most 256 entries have the same value of pair_targets // 128, and every device's list reaches this many for some value. `node_counts`: each drop's counts sum to 642.
All inputs are finite; a program needn't handle non-finite values.
Results may differ from the reference program's by a relative error of at most 0.0003.
Values sent between devices are 32-bit elements; how exact they have to be, the bound alone decides.
A program may use at most 64 MiB of HBM per device.

```python
import math
import jax
import jax.numpy as jnp
import numpy as np
from jax import lax

P_SIZE = 128
CPD = 8
NODES_DROP = 642
CL_DEV = 128
PAIRS_DEV = 512
DEVS = 16
CLUSTERS = 2048
DROP_DEV = 16
DROPS = 256
CAP = 16
TCAP = 256
N_ROW = 4
N_COL = 4


def cluster_layout(key):
    base = jax.random.fold_in(key, 7)
    first_key, second_key, third_key = jax.random.split(base, 3)
    group_count = CL_DEV // CAP
    ranking = jax.random.permutation(first_key, DEVS).astype(jnp.int32)
    ranking = ranking.at[1].set(-2)
    ranking = ranking.at[DEVS // 2].set(-1)
    offsets = jnp.argsort(ranking, stable=True)[:group_count].astype(jnp.int32)
    owners = jnp.arange(DEVS, dtype=jnp.int32)[:, None]
    arrival = jnp.arange(CL_DEV, dtype=jnp.int32)[None, :]
    group_of = arrival // CAP
    anchor = (owners - offsets[group_of]) % DEVS
    homes = anchor * CL_DEV + arrival
    shuffle_keys = jax.random.split(second_key, DEVS)
    shuffles = jax.vmap(lambda one_key: jax.random.permutation(one_key, CL_DEV))(shuffle_keys)
    homes = jnp.take_along_axis(homes, shuffles.astype(jnp.int32), axis=1)
    grouped = homes.reshape(DEVS * DROP_DEV, CPD)
    labels = jax.random.permutation(third_key, DROPS).astype(jnp.int32)
    clusters = jnp.zeros((DROPS, CPD), jnp.int32).at[labels].set(grouped)
    owner_of = jnp.zeros((DROPS,), jnp.int32).at[labels].set(jnp.arange(DROPS, dtype=jnp.int32) // DROP_DEV)
    return (clusters, owner_of)


def draw_drop_clusters(key, part):
    return cluster_layout(key)[0]


def draw_drop_owner(key, part):
    return cluster_layout(key)[1]


def draw_pair_count(key, part):
    base = jax.random.fold_in(key, 11)
    first_key, second_key = jax.random.split(base, 2)
    counts = jax.random.randint(first_key, (DEVS,), PAIRS_DEV // 8, PAIRS_DEV // 2 + 1, dtype=jnp.int32)
    busiest = jax.random.randint(second_key, (), 0, DEVS, dtype=jnp.int32)
    return counts.at[busiest].set(PAIRS_DEV)


def draw_pair_targets(key, part):
    base = jax.random.fold_in(key, 13)
    first_key, second_key, third_key = jax.random.split(base, 3)
    perm_keys = jax.random.split(first_key, DEVS)
    orders = jax.vmap(lambda one_key: jax.random.permutation(one_key, PAIRS_DEV))(perm_keys).astype(jnp.int32)
    shifts = jax.random.randint(second_key, (DEVS, 1), 0, N_COL, dtype=jnp.int32)
    home_col = (orders // TCAP + shifts) % N_COL
    within = jax.random.randint(third_key, (DEVS, PAIRS_DEV), 0, CL_DEV, dtype=jnp.int32)
    return home_col * CL_DEV + within


def place_ends(values, stream_key, low, largest):
    index_at = [jax.random.randint(jax.random.fold_in(stream_key, axis), (), 0, length) for axis, length in enumerate(values.shape)]
    main_axis = values.shape.index(max(values.shape))
    neighbour = index_at[:main_axis] + [(index_at[main_axis] + 1) % values.shape[main_axis]] + index_at[main_axis + 1:]
    return values.at[tuple(index_at)].set(low).at[tuple(neighbour)].set(largest)


def level_of(own_key, shape, pieces, smallest, high):
    def one(axis_at, shards_of):
        steps = jax.random.uniform(jax.random.fold_in(jax.random.fold_in(own_key, 6), axis_at), (shards_of,), jnp.float32, smallest / len(pieces), high / len(pieces))
        return jnp.repeat(jnp.exp(steps), shape[axis_at] // shards_of).reshape((-1,) + (1,) * (len(shape) - axis_at - 1))

    loudness = one(*pieces[0])
    for cut in pieces[1:]:
        loudness = loudness * one(*cut)
    return loudness


def length_profile(count, total, most, slope):
    portions = [(1 << 20) // math.isqrt(grade ** slope) + 1 for grade in range(2, count + 1)]
    surplus, given = total - most - (count - 1), [1] * (count - 1)
    while surplus > 0:
        free = [i for i in range(count - 1) if given[i] < most]
        mass, left = sum([portions[i] for i in free]), surplus
        for i in free:
            more = min(most - given[i], max(1, left * portions[i] // mass), surplus)
            given[i] = given[i] + more
            surplus = surplus - more
    return np.array([most] + given)


def uneven_parts(stream_key, number_of, total, most, skew):
    if number_of == 2:
        one = jax.random.randint(stream_key, (), max(1, total - most), min(most, total - 1) + 1)
        return jnp.stack([one, total - one])
    tallies = jnp.asarray(length_profile(number_of, total, most, skew), jnp.int32)
    pairs = (number_of - 1) // 2
    source_of, sink = tallies[1:1 + 2 * pairs:2], tallies[2:2 + 2 * pairs:2]
    slack = jnp.minimum(source_of - 1, most - sink)
    moved = jax.random.randint(jax.random.fold_in(stream_key, 1), (pairs,), 0, 1 << 20) % (slack + 1)
    tallies = tallies.at[1:1 + 2 * pairs:2].set(source_of - moved).at[2:2 + 2 * pairs:2].set(sink + moved)
    return tallies[jax.random.permutation(jax.random.fold_in(stream_key, 2), number_of)]


def gaussian(key, extent, deviation, bound, pieces=(), kind=jnp.bfloat16):
    factor_of = level_of(key, extent, pieces, -0.22, 0.18) if pieces else 1.0
    drawn = jax.random.normal(key, extent, jnp.float32) * deviation * factor_of
    return jnp.minimum(jnp.maximum(drawn, -bound), bound).astype(kind)


def setup_inputs(seed: int = 0, part: int = 0) -> dict:
    splits = jax.random.split(jax.random.key(seed), 10)
    part_keys = jax.random.split(jax.random.fold_in(splits[9], part), 10)
    return {
        "positions": gaussian(part_keys[0], (CLUSTERS, 3, P_SIZE), 1.0, 6.0, ((0, 16),), jnp.float32),
        "normals": gaussian(part_keys[1], (CLUSTERS, 3, P_SIZE), 1.0, 6.0, ((0, 16),), jnp.float32),
        "curvature": jnp.clip(0.5 + 2.5 * jax.random.uniform(part_keys[2], (CLUSTERS, P_SIZE), jnp.float32) ** level_of(part_keys[2], (CLUSTERS, P_SIZE), ((0, 16),), -0.2, 0.2), 0.5, 3.0),
        "pair_targets": draw_pair_targets(jax.random.fold_in(jax.random.fold_in(splits[9], part), 71), part),
        "pair_sources": place_ends(jax.random.randint(part_keys[4], (DEVS, PAIRS_DEV), 0, N_ROW * CL_DEV), jax.random.fold_in(part_keys[4], 1), 0, (N_ROW * CL_DEV) - 1).astype(jnp.int32),
        "pair_count": draw_pair_count(jax.random.fold_in(jax.random.fold_in(splits[9], part), 71), part),
        "node_counts": jax.vmap(lambda own: uneven_parts(own, CPD, NODES_DROP, P_SIZE, 1))(jax.random.split(part_keys[6], DROPS)).reshape((DROPS, CPD)).astype(jnp.int32),
        "drop_clusters": draw_drop_clusters(jax.random.fold_in(jax.random.fold_in(splits[9], part), 71), part),
        "drop_owner": draw_drop_owner(jax.random.fold_in(jax.random.fold_in(splits[9], part), 71), part),
    }


pair_block = 32
regular_sq = 0.0025
stokes_scale = 1.0 / (8.0 * math.pi)

def stokeslet(target_pos, source_pos, source_force):
    delta_x = target_pos[:, 0, :, None] - source_pos[:, 0, None, :]
    delta_y = target_pos[:, 1, :, None] - source_pos[:, 1, None, :]
    delta_z = target_pos[:, 2, :, None] - source_pos[:, 2, None, :]
    dist_sq = delta_x * delta_x + delta_y * delta_y + delta_z * delta_z
    inverse = lax.rsqrt(dist_sq + regular_sq)
    weight = inverse * inverse * inverse
    isotropic = (dist_sq + 2.0 * regular_sq) * weight
    force_x = source_force[:, 0, None, :]
    force_y = source_force[:, 1, None, :]
    force_z = source_force[:, 2, None, :]
    project = (delta_x * force_x + delta_y * force_y + delta_z * force_z) * weight
    speed_x = lax.optimization_barrier(jnp.sum(isotropic * force_x + project * delta_x, axis=2))
    speed_y = lax.optimization_barrier(jnp.sum(isotropic * force_y + project * delta_y, axis=2))
    speed_z = lax.optimization_barrier(jnp.sum(isotropic * force_z + project * delta_z, axis=2))
    return stokes_scale * jnp.stack([speed_x, speed_y, speed_z], axis=1)

def reference(positions, normals, curvature, pair_targets, pair_sources, pair_count, node_counts, drop_clusters, drop_owner):
    entries = DROPS * CPD
    flat_clusters = drop_clusters.reshape(-1)
    flat_counts = node_counts.reshape(-1)
    home_counts = jnp.zeros((entries,), jnp.int32).at[flat_clusters].set(flat_counts)
    slot_index = jnp.arange(P_SIZE, dtype=jnp.int32)
    home_live = (slot_index[None, :] < home_counts[:, None]).astype(jnp.float32)
    forces = (curvature * home_live)[:, None, :] * normals
    devices = jnp.arange(DEVS, dtype=jnp.int32)
    row_of = devices // N_COL
    col_of = devices % N_COL
    target_global = row_of[:, None] * (N_COL * CL_DEV) + pair_targets
    source_global = (pair_sources // CL_DEV * N_COL + col_of[:, None]) * CL_DEV + pair_sources % CL_DEV

    def per_device(speeds, items):
        target_row, source_row, limit = items
        blocks = (limit + pair_block - 1) // pair_block

        def accumulate(block_number, totals):
            picked = block_number * pair_block + jnp.arange(pair_block, dtype=jnp.int32)
            active = picked < limit
            picked = jnp.minimum(picked, PAIRS_DEV - 1)
            target_ids = target_row[picked]
            source_ids = source_row[picked]
            contrib = stokeslet(positions[target_ids], positions[source_ids], forces[source_ids])
            contrib = contrib * active.astype(jnp.float32)[:, None, None]
            return totals.at[target_ids].add(contrib)
        return (lax.fori_loop(0, blocks, accumulate, speeds), None)
    speeds, unused = lax.scan(per_device, jnp.zeros((entries, 3, P_SIZE), jnp.float32), (target_global, source_global, pair_count))
    owner_order = jnp.argsort(drop_owner, stable=True)
    ordered_clusters = drop_clusters[owner_order].reshape(-1)
    ordered_counts = node_counts[owner_order].reshape(-1)
    owned_live = (slot_index[None, :] < ordered_counts[:, None]).astype(jnp.float32)
    return speeds[ordered_clusters] * owned_live[:, None, :]
```

```python
import functools
import math

import jax
import jax.numpy as jnp
from jax import lax
from jax.experimental import pallas as pl
from jax.experimental.pallas import tpu as pltpu
from jax.sharding import PartitionSpec as P

regular_sq = 0.0025
stokes_scale = 1.0 / (8.0 * math.pi)
MESH = pl.DeviceIdType.MESH
VMEM = pl.BlockSpec(memory_space=pltpu.VMEM)
SMEM = pl.BlockSpec(memory_space=pltpu.SMEM)


def gather_kernel(nrow, ncol, pos_ref, nrm_ref, curv_ref, cnt_ref, t_ref, s_ref, tsend, trecv, ssend, srecv):
    row, col = lax.axis_index("row"), lax.axis_index("col")
    local = pos_ref.shape[0]
    barrier = pltpu.get_barrier_semaphore()
    for d in range(1, nrow):
        pl.semaphore_signal(barrier, inc=1, device_id={"row": lax.rem(row + d, nrow)}, device_id_type=MESH)
    for d in range(1, ncol):
        pl.semaphore_signal(barrier, inc=1, device_id={"col": lax.rem(col + d, ncol)}, device_id_type=MESH)
    tmine = pl.ds(pl.multiple_of(col * local, local), local)
    smine = pl.ds(pl.multiple_of(row * local, local), local)
    live = lax.broadcasted_iota(jnp.int32, curv_ref.shape, 1) < cnt_ref[...]
    scale = jnp.where(live, curv_ref[...], 0.0)
    for k in range(3):
        coord = pos_ref[:, k, :]
        t_ref[k, tmine, :] = coord
        s_ref[k, smine, :] = coord
        s_ref[3 + k, smine, :] = scale * nrm_ref[:, k, :]
    pl.semaphore_wait(barrier, nrow + ncol - 2)
    copies = []
    for d in range(1, nrow):
        copies.append(pltpu.make_async_remote_copy(
            src_ref=s_ref.at[:, smine, :], dst_ref=s_ref.at[:, smine, :],
            send_sem=ssend.at[d - 1], recv_sem=srecv.at[d - 1],
            device_id={"row": lax.rem(row + d, nrow)}, device_id_type=MESH))
    for d in range(1, ncol):
        copies.append(pltpu.make_async_remote_copy(
            src_ref=t_ref.at[:, tmine, :], dst_ref=t_ref.at[:, tmine, :],
            send_sem=tsend.at[d - 1], recv_sem=trecv.at[d - 1],
            device_id={"col": lax.rem(col + d, ncol)}, device_id_type=MESH))
    for copy in copies:
        copy.start()
    for copy in copies:
        copy.wait()


def pair_kernel(tgt_ref, src_ref, count_ref, t_ref, s_ref, v_ref, sc_ref):
    v_ref[...] = jnp.zeros_like(v_ref)
    for k in range(6):
        sc_ref[:, k, :] = s_ref[k]
    step = 32

    def one(e, carry):
        t, s = tgt_ref[0, e], src_ref[0, e]
        tx, ty, tz = (t_ref[k, pl.ds(t, 1), :] for k in range(3))
        turned = sc_ref[s].T
        total = [jnp.zeros((8, 128), jnp.float32) for _ in range(3)]
        for i in range(128 // step):
            part = turned[i * step:(i + 1) * step]
            dx, dy, dz = tx - part[:, 0:1], ty - part[:, 1:2], tz - part[:, 2:3]
            fx, fy, fz = part[:, 3:4], part[:, 4:5], part[:, 5:6]
            inv = lax.rsqrt(dx * dx + dy * dy + dz * dz + regular_sq)
            weight = inv * inv * inv
            iso = inv + regular_sq * weight
            proj = (dx * fx + dy * fy + dz * fz) * weight
            for k, (f, w) in enumerate(((fx, dx), (fy, dy), (fz, dz))):
                total[k] += (iso * f + proj * w).reshape(step // 8, 8, 128).sum(axis=0)
        for k in range(3):
            v_ref[k, pl.ds(t, 1), :] += stokes_scale * jnp.sum(total[k], axis=0, keepdims=True)
        return carry

    lax.fori_loop(0, count_ref[0], one, 0)


def home_kernel(nrow, ncol, cap, pack_ref, unpack_ref, cnt_ref, v_ref, out_ref, got, home, outg, arr, vsend, vrecv, asend, arecv):
    row, col = lax.axis_index("row"), lax.axis_index("col")
    local = out_ref.shape[0]
    devs = nrow * ncol
    me = row * ncol + col
    barrier = pltpu.get_barrier_semaphore()

    def peer(d):
        p = lax.rem(me + d, devs)
        return {"row": p // ncol, "col": lax.rem(p, ncol)}

    for d in range(1, devs):
        pl.semaphore_signal(barrier, inc=1, device_id=peer(d), device_id_type=MESH)
    pl.semaphore_wait(barrier, devs - 1)
    copies = []
    for d in range(1, ncol):
        to = lax.rem(col + d, ncol)
        copies.append(pltpu.make_async_remote_copy(
            src_ref=v_ref.at[:, pl.ds(pl.multiple_of(to * local, local), local), :],
            dst_ref=got.at[d - 1], send_sem=vsend.at[d - 1], recv_sem=vrecv.at[d - 1],
            device_id={"col": to}, device_id_type=MESH))
    for copy in copies:
        copy.start()
    for copy in copies:
        copy.wait()
    for k in range(3):
        mine = v_ref[k, pl.ds(pl.multiple_of(col * local, local), local), :]
        for d in range(1, ncol):
            mine = mine + got[d - 1, k]
        home[:, k, :] = mine

    unroll = 8

    def pack(i, carry):
        for u in range(unroll):
            slot = i * unroll + u
            outg[slot] = home[pack_ref[slot], 0:3, :]
        return carry

    lax.fori_loop(0, devs * cap // unroll, pack, 0)
    copies = []
    own = pl.ds(me * cap, cap)
    for d in range(1, devs):
        p = lax.rem(me + d, devs)
        copies.append(pltpu.make_async_remote_copy(
            src_ref=outg.at[pl.ds(p * cap, cap)], dst_ref=arr.at[own],
            send_sem=asend.at[d - 1], recv_sem=arecv.at[d - 1],
            device_id=peer(d), device_id_type=MESH))
    for copy in copies:
        copy.start()
    arr[own] = outg[own]
    for copy in copies:
        copy.wait()
    slots = lax.broadcasted_iota(jnp.int32, (3, 128), 1)

    def unpack(i, carry):
        for u in range(unroll):
            n = i * unroll + u
            out_ref[n] = jnp.where(slots < cnt_ref[n], arr[unpack_ref[n]], 0.0)
        return carry

    lax.fori_loop(0, local // unroll, unpack, 0)


def per_device(positions, normals, curvature, pair_targets, pair_sources, pair_count, node_counts, drop_clusters, drop_owner):
    local, _, nodes = positions.shape
    nrow, ncol = lax.axis_size("row"), lax.axis_size("col")
    devs = nrow * ncol
    me = lax.axis_index("row") * ncol + lax.axis_index("col")
    cap = max(2, 2 * local // devs)
    per_drop = drop_clusters.shape[1]
    drops = drop_owner.shape[0]
    here = local // per_drop
    ints = jnp.int32

    flat_clusters = drop_clusters.reshape(-1)
    flat_counts = node_counts.reshape(-1)
    flat_owner = jnp.broadcast_to(drop_owner[:, None], (drops, per_drop)).reshape(-1)
    order = jnp.arange(local, dtype=ints)
    hit = (me * local + order)[:, None] == flat_clusters[None, :]
    home_counts = jnp.sum(jnp.where(hit, flat_counts[None, :], 0), axis=1, dtype=ints)
    home_owner = jnp.sum(jnp.where(hit, flat_owner[None, :], 0), axis=1, dtype=ints)
    rank = jnp.sum((home_owner[None, :] == home_owner[:, None]) & (order[None, :] < order[:, None]), axis=1, dtype=ints)
    slot_of = home_owner * cap + rank
    all_slots = jnp.arange(devs * cap, dtype=ints)
    pack = jnp.sum(jnp.where(slot_of[None, :] == all_slots[:, None], order[None, :], 0), axis=1, dtype=ints)

    drop_ids = jnp.arange(drops, dtype=ints)
    mine = drop_owner == me
    place = jnp.sum(mine[None, :] & (drop_ids[None, :] < drop_ids[:, None]), axis=1, dtype=ints)
    chosen = mine[None, :] & (place[None, :] == jnp.arange(here, dtype=ints)[:, None])
    owned_clusters = jnp.sum(jnp.where(chosen[:, :, None], drop_clusters[None], 0), axis=1, dtype=ints).reshape(-1)
    owned_counts = jnp.sum(jnp.where(chosen[:, :, None], node_counts[None], 0), axis=1, dtype=ints).reshape(-1)
    anchor = owned_clusters // local
    before = (anchor[None, :] == anchor[:, None]) & (owned_clusters[None, :] < owned_clusters[:, None])
    unpack = anchor * cap + jnp.sum(before, axis=1, dtype=ints)

    dma = pltpu.SemaphoreType.DMA
    f32 = jnp.float32
    targets, sources = pl.pallas_call(
        functools.partial(gather_kernel, nrow, ncol),
        out_shape=(jax.ShapeDtypeStruct((3, ncol * local, nodes), f32), jax.ShapeDtypeStruct((6, nrow * local, nodes), f32)),
        in_specs=[VMEM] * 4, out_specs=(VMEM, VMEM),
        scratch_shapes=[dma((ncol - 1,)), dma((ncol - 1,)), dma((nrow - 1,)), dma((nrow - 1,))],
        compiler_params=pltpu.CompilerParams(collective_id=0, has_side_effects=True, vmem_limit_bytes=56 << 20),
        name="gather_blocks",
    )(positions, normals, curvature, home_counts[:, None])
    speeds = pl.pallas_call(
        pair_kernel,
        out_shape=jax.ShapeDtypeStruct((3, ncol * local, nodes), f32),
        in_specs=[SMEM] * 3 + [VMEM] * 2, out_specs=VMEM,
        scratch_shapes=[pltpu.VMEM((nrow * local, 8, nodes), f32)],
        compiler_params=pltpu.CompilerParams(vmem_limit_bytes=56 << 20),
        name="pairs",
    )(pair_targets, pair_sources, pair_count, targets, sources)
    return pl.pallas_call(
        functools.partial(home_kernel, nrow, ncol, cap),
        out_shape=jax.ShapeDtypeStruct((local, 3, nodes), f32),
        in_specs=[SMEM] * 3 + [VMEM], out_specs=VMEM,
        scratch_shapes=[
            pltpu.VMEM((ncol - 1, 3, local, nodes), f32), pltpu.VMEM((local, 8, nodes), f32),
            pltpu.VMEM((devs * cap, 3, nodes), f32), pltpu.VMEM((devs * cap, 3, nodes), f32),
            dma((ncol - 1,)), dma((ncol - 1,)), dma((devs - 1,)), dma((devs - 1,)),
        ],
        compiler_params=pltpu.CompilerParams(collective_id=1, has_side_effects=True, vmem_limit_bytes=56 << 20),
        name="to_owners",
    )(pack, unpack, owned_counts, speeds)


def solution(mesh):
    every = ("groups", "row", "col")
    in_specs = (
        P(every, None, None), P(every, None, None), P(every, None), P(every, None), P(every, None), P(every),
        P("groups", None), P("groups", None), P("groups"),
    )
    return jax.shard_map(per_device, mesh=mesh, in_specs=in_specs, out_specs=P(every, None, None), check_vma=False)
```

```python
import functools
import math

import jax
import jax.numpy as jnp
from jax import lax
from jax.experimental import pallas as pl
from jax.experimental.pallas import tpu as pltpu
from jax.sharding import PartitionSpec as P

regular_sq = 0.0025
stokes_scale = 1.0 / (8.0 * math.pi)
MESH = pl.DeviceIdType.MESH
VMEM = pl.BlockSpec(memory_space=pltpu.VMEM)
SMEM = pl.BlockSpec(memory_space=pltpu.SMEM)


unroll = 4


def gather_kernel(nrow, ncol, pos_ref, nrm_ref, curv_ref, cnt_ref, t_ref, s_ref, tsend, trecv, ssend, srecv):
    row, col = lax.axis_index("row"), lax.axis_index("col")
    barrier = pltpu.get_barrier_semaphore()
    for d in range(1, nrow):
        pl.semaphore_signal(barrier, inc=1, device_id={"row": lax.rem(row + d, nrow)}, device_id_type=MESH)
    for d in range(1, ncol):
        pl.semaphore_signal(barrier, inc=1, device_id={"col": lax.rem(col + d, ncol)}, device_id_type=MESH)
    live = lax.broadcasted_iota(jnp.int32, curv_ref.shape, 1) < cnt_ref[...]
    scale = jnp.where(live, curv_ref[...], 0.0)
    for k in range(3):
        coord = pos_ref[:, k, :]
        t_ref[col, k] = coord
        s_ref[row, k] = coord
        s_ref[row, 3 + k] = scale * nrm_ref[:, k, :]
    pl.semaphore_wait(barrier, nrow + ncol - 2)
    copies = []
    for d in range(1, nrow):
        copies.append(pltpu.make_async_remote_copy(
            src_ref=s_ref.at[row], dst_ref=s_ref.at[row],
            send_sem=ssend.at[d - 1], recv_sem=srecv.at[d - 1],
            device_id={"row": lax.rem(row + d, nrow)}, device_id_type=MESH))
    for d in range(1, ncol):
        copies.append(pltpu.make_async_remote_copy(
            src_ref=t_ref.at[col], dst_ref=t_ref.at[col],
            send_sem=tsend.at[d - 1], recv_sem=trecv.at[d - 1],
            device_id={"col": lax.rem(col + d, ncol)}, device_id_type=MESH))
    for copy in copies:
        copy.start()
    for copy in copies:
        copy.wait()


def split3(x):
    high = x.astype(jnp.bfloat16).astype(jnp.float32)
    rest = x - high
    middle = rest.astype(jnp.bfloat16).astype(jnp.float32)
    return high, middle, rest - middle


def split2(x):
    high = x.astype(jnp.bfloat16)
    return high, (x - high.astype(jnp.float32)).astype(jnp.bfloat16)


def pair_kernel(tgt_ref, src_ref, count_ref, t_ref, s_ref, v_ref, tc_ref, sc_ref):
    ncol, _, local, _ = t_ref.shape
    nrow = s_ref.shape[0]
    slots = tgt_ref.shape[1]
    f32 = jnp.float32
    v_ref[...] = jnp.zeros_like(v_ref)

    def targets(c, carry):
        rows = pl.ds(pl.multiple_of(c * local, local), local)
        square = jnp.full((local, 128), regular_sq, f32)
        for k in range(3):
            coord = t_ref[c, k]
            centre = jnp.mean(coord, axis=1, keepdims=True)
            coord = coord - centre
            square = square + coord * coord
            tc_ref[rows, k, :] = coord
            tc_ref[rows, 5 + k, :] = jnp.broadcast_to(centre, coord.shape)
        tc_ref[rows, 3, :] = square
        tc_ref[rows, 4, :] = jnp.ones((local, 128), f32)
        return carry

    lax.fori_loop(0, ncol, targets, 0)

    def sources(r, carry):
        rows = pl.ds(pl.multiple_of(r * local, local), local)
        for k in range(6):
            sc_ref[rows, k, :] = s_ref[r, k]
        return carry

    lax.fori_loop(0, nrow, sources, 0)
    count = count_ref[0]
    ones = jnp.ones((1, 128), f32)
    none = jnp.zeros((3, 128), f32)

    def many(block, carry):
        made = []
        for u in range(unroll):
            e = block * unroll + u
            active = e < count
            e = jnp.minimum(e, slots - 1)
            t, s = tgt_ref[0, e], src_ref[0, e]
            near = tc_ref[t]
            far = sc_ref[s]
            shifted = far[0:3] - near[5:8]
            force = jnp.where(active, far[3:6], 0.0)
            square = jnp.sum(shifted * shifted, axis=0, keepdims=True)
            along = jnp.sum(shifted * force, axis=0, keepdims=True)
            a_hi, a_mid, a_lo = split3(jnp.concatenate([near[0:5], none], axis=0))
            b_hi, b_mid, b_lo = split3(jnp.concatenate([-2.0 * shifted, ones, square, none], axis=0))
            c_hi, c_mid, c_lo = split3(jnp.concatenate([force, 0.0 * ones, -along, none], axis=0))
            right = jnp.concatenate([a_hi, a_mid, a_lo, a_hi, a_mid, a_hi], axis=0).astype(jnp.bfloat16)
            left = jnp.concatenate([
                jnp.concatenate([b_hi, b_hi, b_hi, b_mid, b_mid, b_lo], axis=0),
                jnp.concatenate([c_hi, c_hi, c_hi, c_mid, c_mid, c_lo], axis=0)], axis=1).astype(jnp.bfloat16)
            both = lax.dot_general(left, right, (((0,), (0,)), ((), ())), preferred_element_type=f32)
            gathered = jnp.concatenate([force, shifted, ones, ones], axis=0)
            g_hi = gathered.astype(jnp.bfloat16).astype(f32)
            g = jnp.concatenate([g_hi, gathered - g_hi], axis=0).astype(jnp.bfloat16)
            made.append((t, near, both, g))
        results = []
        for t, near, both, g in made:
            inv = lax.rsqrt(both[0:128])
            weight = inv * inv * inv
            iso_hi, iso_lo = split2(inv + regular_sq * weight)
            pro_hi, pro_lo = split2(both[128:256] * weight)
            m = jnp.concatenate([
                jnp.concatenate([iso_hi, pro_hi], axis=1), jnp.concatenate([iso_lo, pro_lo], axis=1)], axis=0)
            out = jnp.dot(jnp.concatenate([g, g], axis=1), m, preferred_element_type=f32)
            out = out[0:8] + out[8:16]
            results.append((t, stokes_scale * (out[0:3, 0:128] + near[0:3] * out[6:7, 128:256] - out[3:6, 128:256])))
        for t, speed in results:
            c, i = t // local, lax.rem(t, local)
            for k in range(3):
                v_ref[c, k, pl.ds(i, 1), :] += speed[k:k + 1]
        return carry

    lax.fori_loop(0, (count + unroll - 1) // unroll, many, 0)


def home_kernel(nrow, ncol, cap, pack_ref, unpack_ref, cnt_ref, v_ref, out_ref, got, home, outg, arr, vsend, vrecv, asend, arecv):
    row, col = lax.axis_index("row"), lax.axis_index("col")
    local = out_ref.shape[0]
    devs = nrow * ncol
    me = row * ncol + col
    barrier = pltpu.get_barrier_semaphore()

    def peer(d):
        p = lax.rem(me + d, devs)
        return {"row": p // ncol, "col": lax.rem(p, ncol)}

    for d in range(1, devs):
        pl.semaphore_signal(barrier, inc=1, device_id=peer(d), device_id_type=MESH)
    pl.semaphore_wait(barrier, devs - 1)
    copies = []
    for d in range(1, ncol):
        to = lax.rem(col + d, ncol)
        copies.append(pltpu.make_async_remote_copy(
            src_ref=v_ref.at[to], dst_ref=got.at[d - 1], send_sem=vsend.at[d - 1], recv_sem=vrecv.at[d - 1],
            device_id={"col": to}, device_id_type=MESH))
    for copy in copies:
        copy.start()
    for copy in copies:
        copy.wait()
    for k in range(3):
        mine = v_ref[col, k]
        for d in range(1, ncol):
            mine = mine + got[d - 1, k]
        home[:, k, :] = mine

    def pack(p, carry):
        for j in range(cap):
            one = home[pack_ref[p * cap + j]]
            for k in range(3):
                outg[p, k, j:j + 1, :] = one[k:k + 1]
        return carry

    lax.fori_loop(0, devs, pack, 0)
    copies = []
    for d in range(1, devs):
        copies.append(pltpu.make_async_remote_copy(
            src_ref=outg.at[lax.rem(me + d, devs)], dst_ref=arr.at[me],
            send_sem=asend.at[d - 1], recv_sem=arecv.at[d - 1],
            device_id=peer(d), device_id_type=MESH))
    for copy in copies:
        copy.start()
    arr[me] = outg[me]
    for copy in copies:
        copy.wait()
    slots = lax.broadcasted_iota(jnp.int32, (1, 128), 1)

    def unpack(i, carry):
        for u in range(8):
            n = i * 8 + u
            at = unpack_ref[n]
            live = slots < cnt_ref[n]
            for k in range(3):
                out_ref[n, k:k + 1, :] = jnp.where(live, arr[at // cap, k, pl.ds(lax.rem(at, cap), 1), :], 0.0)
        return carry

    lax.fori_loop(0, local // 8, unpack, 0)


def per_device(positions, normals, curvature, pair_targets, pair_sources, pair_count, node_counts, drop_clusters, drop_owner):
    local, _, nodes = positions.shape
    nrow, ncol = lax.axis_size("row"), lax.axis_size("col")
    devs = nrow * ncol
    me = lax.axis_index("row") * ncol + lax.axis_index("col")
    cap = max(2, 2 * local // devs)
    per_drop = drop_clusters.shape[1]
    drops = drop_owner.shape[0]
    here = local // per_drop
    ints = jnp.int32

    flat_clusters = drop_clusters.reshape(-1)
    flat_counts = node_counts.reshape(-1)
    flat_owner = jnp.broadcast_to(drop_owner[:, None], (drops, per_drop)).reshape(-1)
    order = jnp.arange(local, dtype=ints)
    hit = (me * local + order)[:, None] == flat_clusters[None, :]
    home_counts = jnp.sum(jnp.where(hit, flat_counts[None, :], 0), axis=1, dtype=ints)
    home_owner = jnp.sum(jnp.where(hit, flat_owner[None, :], 0), axis=1, dtype=ints)
    rank = jnp.sum((home_owner[None, :] == home_owner[:, None]) & (order[None, :] < order[:, None]), axis=1, dtype=ints)
    slot_of = home_owner * cap + rank
    all_slots = jnp.arange(devs * cap, dtype=ints)
    pack = jnp.sum(jnp.where(slot_of[None, :] == all_slots[:, None], order[None, :], 0), axis=1, dtype=ints)

    drop_ids = jnp.arange(drops, dtype=ints)
    mine = drop_owner == me
    place = jnp.sum(mine[None, :] & (drop_ids[None, :] < drop_ids[:, None]), axis=1, dtype=ints)
    chosen = mine[None, :] & (place[None, :] == jnp.arange(here, dtype=ints)[:, None])
    owned_clusters = jnp.sum(jnp.where(chosen[:, :, None], drop_clusters[None], 0), axis=1, dtype=ints).reshape(-1)
    owned_counts = jnp.sum(jnp.where(chosen[:, :, None], node_counts[None], 0), axis=1, dtype=ints).reshape(-1)
    anchor = owned_clusters // local
    before = (anchor[None, :] == anchor[:, None]) & (owned_clusters[None, :] < owned_clusters[:, None])
    unpack = anchor * cap + jnp.sum(before, axis=1, dtype=ints)

    dma = pltpu.SemaphoreType.DMA
    f32 = jnp.float32
    targets, sources = pl.pallas_call(
        functools.partial(gather_kernel, nrow, ncol),
        out_shape=(jax.ShapeDtypeStruct((ncol, 3, local, nodes), f32), jax.ShapeDtypeStruct((nrow, 6, local, nodes), f32)),
        in_specs=[VMEM] * 4, out_specs=(VMEM, VMEM),
        scratch_shapes=[dma((ncol - 1,)), dma((ncol - 1,)), dma((nrow - 1,)), dma((nrow - 1,))],
        compiler_params=pltpu.CompilerParams(collective_id=0, has_side_effects=True, vmem_limit_bytes=56 << 20),
        name="gather_blocks",
    )(positions, normals, curvature, home_counts[:, None])
    speeds = pl.pallas_call(
        pair_kernel,
        out_shape=jax.ShapeDtypeStruct((ncol, 3, local, nodes), f32),
        in_specs=[SMEM] * 3 + [VMEM] * 2, out_specs=VMEM,
        scratch_shapes=[pltpu.VMEM((ncol * local, 8, nodes), f32), pltpu.VMEM((nrow * local, 8, nodes), f32)],
        compiler_params=pltpu.CompilerParams(vmem_limit_bytes=56 << 20),
        name="pairs",
    )(pair_targets, pair_sources, pair_count, targets, sources)
    return pl.pallas_call(
        functools.partial(home_kernel, nrow, ncol, cap),
        out_shape=jax.ShapeDtypeStruct((local, 3, nodes), f32),
        in_specs=[SMEM] * 3 + [VMEM], out_specs=VMEM,
        scratch_shapes=[
            pltpu.VMEM((ncol - 1, 3, local, nodes), f32), pltpu.VMEM((local, 8, nodes), f32),
            pltpu.VMEM((devs, 3, cap, nodes), f32), pltpu.VMEM((devs, 3, cap, nodes), f32),
            dma((ncol - 1,)), dma((ncol - 1,)), dma((devs - 1,)), dma((devs - 1,)),
        ],
        compiler_params=pltpu.CompilerParams(collective_id=1, has_side_effects=True, vmem_limit_bytes=56 << 20),
        name="to_owners",
    )(pack, unpack, owned_counts, speeds)


def solution(mesh):
    every = ("groups", "row", "col")
    in_specs = (
        P(every, None, None), P(every, None, None), P(every, None), P(every, None), P(every, None), P(every),
        P("groups", None), P("groups", None), P("groups"),
    )
    return jax.shard_map(per_device, mesh=mesh, in_specs=in_specs, out_specs=P(every, None, None), check_vma=False)
```

```python
import functools
import math

import jax
import jax.numpy as jnp
from jax import lax
from jax.experimental import pallas as pl
from jax.experimental.pallas import tpu as pltpu
from jax.sharding import PartitionSpec as P

regular_sq = 0.0025
stokes_scale = 1.0 / (8.0 * math.pi)
MESH = pl.DeviceIdType.MESH
VMEM = pl.BlockSpec(memory_space=pltpu.VMEM)
SMEM = pl.BlockSpec(memory_space=pltpu.SMEM)


unroll = 16


def gather_kernel(nrow, ncol, pos_ref, nrm_ref, curv_ref, cnt_ref, t_ref, s_ref, tsend, trecv, ssend, srecv):
    row, col = lax.axis_index("row"), lax.axis_index("col")
    barrier = pltpu.get_barrier_semaphore()
    for d in range(1, nrow):
        pl.semaphore_signal(barrier, inc=1, device_id={"row": lax.rem(row + d, nrow)}, device_id_type=MESH)
    for d in range(1, ncol):
        pl.semaphore_signal(barrier, inc=1, device_id={"col": lax.rem(col + d, ncol)}, device_id_type=MESH)
    live = lax.broadcasted_iota(jnp.int32, curv_ref.shape, 1) < cnt_ref[...]
    scale = jnp.where(live, curv_ref[...], 0.0)
    for k in range(3):
        coord = pos_ref[:, k, :]
        t_ref[col, k] = coord
        s_ref[row, k] = coord
        s_ref[row, 3 + k] = scale * nrm_ref[:, k, :]
    pl.semaphore_wait(barrier, nrow + ncol - 2)
    copies = []
    for d in range(1, ncol):
        copies.append(pltpu.make_async_remote_copy(
            src_ref=t_ref.at[col], dst_ref=t_ref.at[col],
            send_sem=tsend.at[d - 1], recv_sem=trecv.at[d - 1],
            device_id={"col": lax.rem(col + d, ncol)}, device_id_type=MESH))

    def relay(way, step):
        block = jnp.clip(row - way * step, 0, nrow - 1)
        to = jnp.clip(row + way, 0, nrow - 1)
        at = step if way > 0 else nrow - 1 + step
        return pltpu.make_async_remote_copy(
            src_ref=s_ref.at[block], dst_ref=s_ref.at[block],
            send_sem=ssend.at[at], recv_sem=srecv.at[at],
            device_id={"row": to}, device_id_type=MESH)

    def sends(way, step):
        return (row < nrow - 1) & (row >= step) if way > 0 else (row > 0) & (row + step < nrow)

    def receives(way, step):
        return row >= step + 1 if way > 0 else row + step + 1 < nrow

    for step in range(nrow - 1):
        for way in (1, -1):
            if step > 0:
                @pl.when(receives(way, step - 1))
                def _():
                    relay(way, step - 1).wait_recv()

            @pl.when(sends(way, step))
            def _():
                relay(way, step).start()
        if step == 0:
            for copy in copies:
                copy.start()
    for way in (1, -1):
        @pl.when(receives(way, nrow - 2))
        def _():
            relay(way, nrow - 2).wait_recv()
        for step in range(nrow - 1):
            @pl.when(sends(way, step))
            def _():
                relay(way, step).wait_send()
    for copy in copies:
        copy.wait()


def split3(x):
    high = x.astype(jnp.bfloat16).astype(jnp.float32)
    rest = x - high
    middle = rest.astype(jnp.bfloat16).astype(jnp.float32)
    return high, middle, rest - middle


def split2(x):
    high = x.astype(jnp.bfloat16)
    return high, (x - high.astype(jnp.float32)).astype(jnp.bfloat16)


def pair_kernel(tgt_ref, src_ref, count_ref, t_ref, s_ref, v_ref, tc_ref, sc_ref):
    ncol, _, local, _ = t_ref.shape
    nrow = s_ref.shape[0]
    slots = tgt_ref.shape[1]
    f32 = jnp.float32
    v_ref[...] = jnp.zeros_like(v_ref)

    def targets(c, carry):
        rows = pl.ds(pl.multiple_of(c * local, local), local)
        square = jnp.full((local, 128), regular_sq, f32)
        for k in range(3):
            coord = t_ref[c, k]
            centre = jnp.mean(coord, axis=1, keepdims=True)
            coord = coord - centre
            square = square + coord * coord
            tc_ref[rows, k, :] = coord
            tc_ref[rows, 5 + k, :] = jnp.broadcast_to(centre, coord.shape)
        tc_ref[rows, 3, :] = square
        tc_ref[rows, 4, :] = jnp.ones((local, 128), f32)
        return carry

    lax.fori_loop(0, ncol, targets, 0)

    def sources(r, carry):
        rows = pl.ds(pl.multiple_of(r * local, local), local)
        for k in range(6):
            sc_ref[rows, k, :] = s_ref[r, k]
        return carry

    lax.fori_loop(0, nrow, sources, 0)
    count = count_ref[0]
    ones = jnp.ones((1, 128), f32)
    none = jnp.zeros((3, 128), f32)

    def many(block, carry):
        made = []
        for u in range(unroll):
            e = block * unroll + u
            active = e < count
            e = jnp.minimum(e, slots - 1)
            t, s = tgt_ref[0, e], src_ref[0, e]
            near = tc_ref[t]
            far = sc_ref[s]
            shifted = far[0:3] - near[5:8]
            force = jnp.where(active, far[3:6], 0.0)
            square = jnp.sum(shifted * shifted, axis=0, keepdims=True)
            along = jnp.sum(shifted * force, axis=0, keepdims=True)
            a_hi, a_mid, a_lo = split3(jnp.concatenate([near[0:5], none], axis=0))
            b_hi, b_mid, b_lo = split3(jnp.concatenate([-2.0 * shifted, ones, square, none], axis=0))
            c_hi, c_mid, c_lo = split3(jnp.concatenate([force, 0.0 * ones, -along, none], axis=0))
            right = jnp.concatenate([a_hi, a_mid, a_lo, a_hi, a_mid, a_hi], axis=0).astype(jnp.bfloat16)
            left = jnp.concatenate([
                jnp.concatenate([b_hi, b_hi, b_hi, b_mid, b_mid, b_lo], axis=0),
                jnp.concatenate([c_hi, c_hi, c_hi, c_mid, c_mid, c_lo], axis=0)], axis=1).astype(jnp.bfloat16)
            both = lax.dot_general(left, right, (((0,), (0,)), ((), ())), preferred_element_type=f32)
            gathered = jnp.concatenate([force, shifted, ones, ones], axis=0)
            g_hi = gathered.astype(jnp.bfloat16).astype(f32)
            g = jnp.concatenate([g_hi, gathered - g_hi], axis=0).astype(jnp.bfloat16)
            made.append((t, near, both, g))
        results = []
        for t, near, both, g in made:
            inv = lax.rsqrt(both[0:128])
            weight = inv * inv * inv
            iso_hi, iso_lo = split2(inv + regular_sq * weight)
            pro_hi, pro_lo = split2(both[128:256] * weight)
            m = jnp.concatenate([
                jnp.concatenate([iso_hi, pro_hi], axis=1), jnp.concatenate([iso_lo, pro_lo], axis=1)], axis=0)
            out = jnp.dot(jnp.concatenate([g, g], axis=1), m, preferred_element_type=f32)
            out = out[0:8] + out[8:16]
            results.append((t, stokes_scale * (out[0:3, 0:128] + near[0:3] * out[6:7, 128:256] - out[3:6, 128:256])))
        for t, speed in results:
            c, i = t // local, lax.rem(t, local)
            for k in range(3):
                v_ref[c, k, pl.ds(i, 1), :] += speed[k:k + 1]
        return carry

    lax.fori_loop(0, (count + unroll - 1) // unroll, many, 0)


def home_kernel(nrow, ncol, cap, pack_ref, unpack_ref, cnt_ref, v_ref, out_ref, got, home, outg, arr, vsend, vrecv, asend, arecv):
    row, col = lax.axis_index("row"), lax.axis_index("col")
    local = out_ref.shape[0]
    devs = nrow * ncol
    me = row * ncol + col
    barrier = pltpu.get_barrier_semaphore()

    def peer(d):
        p = lax.rem(me + d, devs)
        return {"row": p // ncol, "col": lax.rem(p, ncol)}

    for d in range(1, devs):
        pl.semaphore_signal(barrier, inc=1, device_id=peer(d), device_id_type=MESH)
    pl.semaphore_wait(barrier, devs - 1)
    copies = []
    for d in range(1, ncol):
        to = lax.rem(col + d, ncol)
        copies.append(pltpu.make_async_remote_copy(
            src_ref=v_ref.at[to], dst_ref=got.at[d - 1], send_sem=vsend.at[d - 1], recv_sem=vrecv.at[d - 1],
            device_id={"col": to}, device_id_type=MESH))
    for copy in copies:
        copy.start()
    for copy in copies:
        copy.wait()
    for k in range(3):
        mine = v_ref[col, k]
        for d in range(1, ncol):
            mine = mine + got[d - 1, k]
        home[:, k, :] = mine

    def pack(p, carry):
        for j in range(cap):
            one = home[pack_ref[p * cap + j]]
            for k in range(3):
                outg[p, k, j:j + 1, :] = one[k:k + 1]
        return carry

    lax.fori_loop(0, devs, pack, 0)
    copies = []
    for d in range(1, devs):
        copies.append(pltpu.make_async_remote_copy(
            src_ref=outg.at[lax.rem(me + d, devs)], dst_ref=arr.at[me],
            send_sem=asend.at[d - 1], recv_sem=arecv.at[d - 1],
            device_id=peer(d), device_id_type=MESH))
    for copy in copies:
        copy.start()
    arr[me] = outg[me]
    for copy in copies:
        copy.wait()
    slots = lax.broadcasted_iota(jnp.int32, (1, 128), 1)

    def unpack(i, carry):
        for u in range(8):
            n = i * 8 + u
            at = unpack_ref[n]
            live = slots < cnt_ref[n]
            for k in range(3):
                out_ref[n, k:k + 1, :] = jnp.where(live, arr[at // cap, k, pl.ds(lax.rem(at, cap), 1), :], 0.0)
        return carry

    lax.fori_loop(0, local // 8, unpack, 0)


def per_device(positions, normals, curvature, pair_targets, pair_sources, pair_count, node_counts, drop_clusters, drop_owner):
    local, _, nodes = positions.shape
    nrow, ncol = lax.axis_size("row"), lax.axis_size("col")
    devs = nrow * ncol
    me = lax.axis_index("row") * ncol + lax.axis_index("col")
    cap = max(2, 2 * local // devs)
    per_drop = drop_clusters.shape[1]
    drops = drop_owner.shape[0]
    here = local // per_drop
    ints = jnp.int32

    flat_clusters = drop_clusters.reshape(-1)
    flat_counts = node_counts.reshape(-1)
    flat_owner = jnp.broadcast_to(drop_owner[:, None], (drops, per_drop)).reshape(-1)
    order = jnp.arange(local, dtype=ints)
    hit = (me * local + order)[:, None] == flat_clusters[None, :]
    home_counts = jnp.sum(jnp.where(hit, flat_counts[None, :], 0), axis=1, dtype=ints)
    home_owner = jnp.sum(jnp.where(hit, flat_owner[None, :], 0), axis=1, dtype=ints)
    rank = jnp.sum((home_owner[None, :] == home_owner[:, None]) & (order[None, :] < order[:, None]), axis=1, dtype=ints)
    slot_of = home_owner * cap + rank
    all_slots = jnp.arange(devs * cap, dtype=ints)
    pack = jnp.sum(jnp.where(slot_of[None, :] == all_slots[:, None], order[None, :], 0), axis=1, dtype=ints)

    drop_ids = jnp.arange(drops, dtype=ints)
    mine = drop_owner == me
    place = jnp.sum(mine[None, :] & (drop_ids[None, :] < drop_ids[:, None]), axis=1, dtype=ints)
    chosen = mine[None, :] & (place[None, :] == jnp.arange(here, dtype=ints)[:, None])
    owned_clusters = jnp.sum(jnp.where(chosen[:, :, None], drop_clusters[None], 0), axis=1, dtype=ints).reshape(-1)
    owned_counts = jnp.sum(jnp.where(chosen[:, :, None], node_counts[None], 0), axis=1, dtype=ints).reshape(-1)
    anchor = owned_clusters // local
    before = (anchor[None, :] == anchor[:, None]) & (owned_clusters[None, :] < owned_clusters[:, None])
    unpack = anchor * cap + jnp.sum(before, axis=1, dtype=ints)

    dma = pltpu.SemaphoreType.DMA
    f32 = jnp.float32
    targets, sources = pl.pallas_call(
        functools.partial(gather_kernel, nrow, ncol),
        out_shape=(jax.ShapeDtypeStruct((ncol, 3, local, nodes), f32), jax.ShapeDtypeStruct((nrow, 6, local, nodes), f32)),
        in_specs=[VMEM] * 4, out_specs=(VMEM, VMEM),
        scratch_shapes=[dma((ncol - 1,)), dma((ncol - 1,)), dma((2 * nrow - 2,)), dma((2 * nrow - 2,))],
        compiler_params=pltpu.CompilerParams(collective_id=0, has_side_effects=True, vmem_limit_bytes=56 << 20),
        name="gather_blocks",
    )(positions, normals, curvature, home_counts[:, None])
    speeds = pl.pallas_call(
        pair_kernel,
        out_shape=jax.ShapeDtypeStruct((ncol, 3, local, nodes), f32),
        in_specs=[SMEM] * 3 + [VMEM] * 2, out_specs=VMEM,
        scratch_shapes=[pltpu.VMEM((ncol * local, 8, nodes), f32), pltpu.VMEM((nrow * local, 8, nodes), f32)],
        compiler_params=pltpu.CompilerParams(vmem_limit_bytes=56 << 20),
        name="pairs",
    )(pair_targets, pair_sources, pair_count, targets, sources)
    return pl.pallas_call(
        functools.partial(home_kernel, nrow, ncol, cap),
        out_shape=jax.ShapeDtypeStruct((local, 3, nodes), f32),
        in_specs=[SMEM] * 3 + [VMEM], out_specs=VMEM,
        scratch_shapes=[
            pltpu.VMEM((ncol - 1, 3, local, nodes), f32), pltpu.VMEM((local, 8, nodes), f32),
            pltpu.VMEM((devs, 3, cap, nodes), f32), pltpu.VMEM((devs, 3, cap, nodes), f32),
            dma((ncol - 1,)), dma((ncol - 1,)), dma((devs - 1,)), dma((devs - 1,)),
        ],
        compiler_params=pltpu.CompilerParams(collective_id=1, has_side_effects=True, vmem_limit_bytes=56 << 20),
        name="to_owners",
    )(pack, unpack, owned_counts, speeds)


def solution(mesh):
    every = ("groups", "row", "col")
    in_specs = (
        P(every, None, None), P(every, None, None), P(every, None), P(every, None), P(every, None), P(every),
        P("groups", None), P("groups", None), P("groups"),
    )
    return jax.shard_map(per_device, mesh=mesh, in_specs=in_specs, out_specs=P(every, None, None), check_vma=False)
```

```python
import functools
import math

import jax
import jax.numpy as jnp
from jax import lax
from jax.experimental import pallas as pl
from jax.experimental.pallas import tpu as pltpu
from jax.sharding import PartitionSpec as P

regular_sq = 0.0025
stokes_scale = 1.0 / (8.0 * math.pi)
MESH = pl.DeviceIdType.MESH
VMEM = pl.BlockSpec(memory_space=pltpu.VMEM)
SMEM = pl.BlockSpec(memory_space=pltpu.SMEM)


unroll = 32


def gather_kernel(nrow, ncol, pos_ref, nrm_ref, curv_ref, cnt_ref, t_ref, s_ref, tsend, trecv, ssend, srecv):
    row, col = lax.axis_index("row"), lax.axis_index("col")
    barrier = pltpu.get_barrier_semaphore()
    for d in range(1, nrow):
        pl.semaphore_signal(barrier, inc=1, device_id={"row": lax.rem(row + d, nrow)}, device_id_type=MESH)
    for d in range(1, ncol):
        pl.semaphore_signal(barrier, inc=1, device_id={"col": lax.rem(col + d, ncol)}, device_id_type=MESH)
    live = lax.broadcasted_iota(jnp.int32, curv_ref.shape, 1) < cnt_ref[...]
    scale = jnp.where(live, curv_ref[...], 0.0)
    for k in range(3):
        coord = pos_ref[:, k, :]
        t_ref[col, k] = coord
        s_ref[row, k] = coord
        s_ref[row, 3 + k] = scale * nrm_ref[:, k, :]
    pl.semaphore_wait(barrier, nrow + ncol - 2)
    copies = []
    for d in range(1, ncol):
        copies.append(pltpu.make_async_remote_copy(
            src_ref=t_ref.at[col], dst_ref=t_ref.at[col],
            send_sem=tsend.at[d - 1], recv_sem=trecv.at[d - 1],
            device_id={"col": lax.rem(col + d, ncol)}, device_id_type=MESH))

    def relay(way, step):
        block = jnp.clip(row - way * step, 0, nrow - 1)
        to = jnp.clip(row + way, 0, nrow - 1)
        at = step if way > 0 else nrow - 1 + step
        return pltpu.make_async_remote_copy(
            src_ref=s_ref.at[block], dst_ref=s_ref.at[block],
            send_sem=ssend.at[at], recv_sem=srecv.at[at],
            device_id={"row": to}, device_id_type=MESH)

    def sends(way, step):
        return (row < nrow - 1) & (row >= step) if way > 0 else (row > 0) & (row + step < nrow)

    def receives(way, step):
        return row >= step + 1 if way > 0 else row + step + 1 < nrow

    for step in range(nrow - 1):
        for way in (1, -1):
            if step > 0:
                @pl.when(receives(way, step - 1))
                def _():
                    relay(way, step - 1).wait_recv()

            @pl.when(sends(way, step))
            def _():
                relay(way, step).start()
        if step == 0:
            for copy in copies:
                copy.start()
    for way in (1, -1):
        @pl.when(receives(way, nrow - 2))
        def _():
            relay(way, nrow - 2).wait_recv()
        for step in range(nrow - 1):
            @pl.when(sends(way, step))
            def _():
                relay(way, step).wait_send()
    for copy in copies:
        copy.wait()


def split3(x):
    high = x.astype(jnp.bfloat16).astype(jnp.float32)
    rest = x - high
    middle = rest.astype(jnp.bfloat16).astype(jnp.float32)
    return high, middle, rest - middle


def split2(x):
    high = x.astype(jnp.bfloat16)
    return high, (x - high.astype(jnp.float32)).astype(jnp.bfloat16)


def pair_kernel(tgt_ref, src_ref, count_ref, t_ref, s_ref, v_ref, tc_ref, sc_ref):
    ncol, _, local, _ = t_ref.shape
    nrow = s_ref.shape[0]
    slots = tgt_ref.shape[1]
    f32 = jnp.float32
    v_ref[...] = jnp.zeros_like(v_ref)

    def targets(c, carry):
        rows = pl.ds(pl.multiple_of(c * local, local), local)
        square = jnp.full((local, 128), regular_sq, f32)
        for k in range(3):
            coord = t_ref[c, k]
            centre = jnp.mean(coord, axis=1, keepdims=True)
            coord = coord - centre
            square = square + coord * coord
            tc_ref[rows, k, :] = coord
            tc_ref[rows, 5 + k, :] = jnp.broadcast_to(centre, coord.shape)
        tc_ref[rows, 3, :] = square
        tc_ref[rows, 4, :] = jnp.ones((local, 128), f32)
        return carry

    lax.fori_loop(0, ncol, targets, 0)

    def sources(r, carry):
        rows = pl.ds(pl.multiple_of(r * local, local), local)
        for k in range(6):
            sc_ref[rows, k, :] = s_ref[r, k]
        return carry

    lax.fori_loop(0, nrow, sources, 0)
    count = count_ref[0]
    ones = jnp.ones((1, 128), f32)
    none = jnp.zeros((3, 128), f32)

    def many(block, carry):
        made = []
        for u in range(unroll):
            e = block * unroll + u
            active = e < count
            e = jnp.minimum(e, slots - 1)
            t, s = tgt_ref[0, e], src_ref[0, e]
            near = tc_ref[t]
            far = sc_ref[s]
            shifted = far[0:3] - near[5:8]
            force = jnp.where(active, far[3:6], 0.0)
            square = jnp.sum(shifted * shifted, axis=0, keepdims=True)
            along = jnp.sum(shifted * force, axis=0, keepdims=True)
            a_hi, a_mid, a_lo = split3(jnp.concatenate([near[0:5], none], axis=0))
            b_hi, b_mid, b_lo = split3(jnp.concatenate([-2.0 * shifted, ones, square, none], axis=0))
            c_hi, c_mid, c_lo = split3(jnp.concatenate([force, 0.0 * ones, -along, none], axis=0))
            right = jnp.concatenate([a_hi, a_mid, a_lo, a_hi, a_mid, a_hi], axis=0).astype(jnp.bfloat16)
            left = jnp.concatenate([
                jnp.concatenate([b_hi, b_hi, b_hi, b_mid, b_mid, b_lo], axis=0),
                jnp.concatenate([c_hi, c_hi, c_hi, c_mid, c_mid, c_lo], axis=0)], axis=1).astype(jnp.bfloat16)
            both = lax.dot_general(left, right, (((0,), (0,)), ((), ())), preferred_element_type=f32)
            gathered = jnp.concatenate([force, shifted, ones, ones], axis=0)
            g_hi = gathered.astype(jnp.bfloat16).astype(f32)
            g = jnp.concatenate([g_hi, gathered - g_hi], axis=0).astype(jnp.bfloat16)
            made.append((t, near, both, g))
        results = []
        for t, near, both, g in made:
            inv = lax.rsqrt(both[0:128])
            weight = inv * inv * inv
            iso_hi, iso_lo = split2(inv + regular_sq * weight)
            pro_hi, pro_lo = split2(both[128:256] * weight)
            m = jnp.concatenate([
                jnp.concatenate([iso_hi, pro_hi], axis=1), jnp.concatenate([iso_lo, pro_lo], axis=1)], axis=0)
            out = jnp.dot(jnp.concatenate([g, g], axis=1), m, preferred_element_type=f32)
            out = out[0:8] + out[8:16]
            results.append((t, stokes_scale * (out[0:3, 0:128] + near[0:3] * out[6:7, 128:256] - out[3:6, 128:256])))
        for t, speed in results:
            c, i = t // local, lax.rem(t, local)
            for k in range(3):
                v_ref[c, k, pl.ds(i, 1), :] += speed[k:k + 1]
        return carry

    lax.fori_loop(0, (count + unroll - 1) // unroll, many, 0)


def home_kernel(nrow, ncol, cap, pack_ref, from_ref, rank_ref, cnt_ref, v_ref, out_ref, got, part, home, outg, arr, vsend, vrecv, asend, arecv):
    row, col = lax.axis_index("row"), lax.axis_index("col")
    local = out_ref.shape[0]
    devs = nrow * ncol
    me = row * ncol + col
    barrier = pltpu.get_barrier_semaphore()

    def peer(d):
        p = lax.rem(me + d, devs)
        return {"row": p // ncol, "col": lax.rem(p, ncol)}

    for d in range(1, devs):
        pl.semaphore_signal(barrier, inc=1, device_id=peer(d), device_id_type=MESH)
    pl.semaphore_wait(barrier, devs - 1)
    half = ncol // 2
    core = lax.rem(col, 2)
    mine_x = col // 2
    within, across = [], []
    for d in [*range(1, half), 0]:
        x = lax.rem(mine_x + d, half)
        within.append(pltpu.make_async_remote_copy(
            src_ref=v_ref.at[2 * x + 1 - core], dst_ref=got.at[d], send_sem=vsend.at[d], recv_sem=vrecv.at[d],
            device_id={"col": col + 1 - 2 * core}, device_id_type=MESH))
    for copy in within:
        copy.start()
    for d in range(1, half):
        to = 2 * lax.rem(mine_x + d, half) + core
        within[d - 1].wait_recv()
        part[d - 1] = v_ref[to] + got[d]
        copy = pltpu.make_async_remote_copy(
            src_ref=part.at[d - 1], dst_ref=got.at[half + d - 1],
            send_sem=vsend.at[half + d - 1], recv_sem=vrecv.at[half + d - 1],
            device_id={"col": to}, device_id_type=MESH)
        copy.start()
        across.append(copy)
    within[half - 1].wait_recv()
    for copy in across:
        copy.wait_recv()
    for k in range(3):
        mine = v_ref[col, k] + got[0, k]
        for d in range(1, half):
            mine = mine + got[half + d - 1, k]
        home[:, k, :] = mine
    for copy in within + across:
        copy.wait_send()

    def pack(p, carry):
        for j in range(cap):
            one = home[pack_ref[p * cap + j]]
            for k in range(3):
                outg[p, k, j:j + 1, :] = one[k:k + 1]
        return carry

    lax.fori_loop(0, devs, pack, 0)
    copies = []
    for d in range(1, devs):
        copies.append(pltpu.make_async_remote_copy(
            src_ref=outg.at[lax.rem(me + d, devs)], dst_ref=arr.at[me],
            send_sem=asend.at[d - 1], recv_sem=arecv.at[d - 1],
            device_id=peer(d), device_id_type=MESH))
    for copy in copies:
        copy.start()
    arr[me] = outg[me]
    for copy in copies:
        copy.wait()
    slots = lax.broadcasted_iota(jnp.int32, (1, 128), 1)

    def unpack(i, carry):
        for u in range(8):
            n = i * 8 + u
            at, place = from_ref[n], rank_ref[n]
            live = slots < cnt_ref[n]
            for k in range(3):
                out_ref[n, k:k + 1, :] = jnp.where(live, arr[at, k, pl.ds(place, 1), :], 0.0)
        return carry

    lax.fori_loop(0, local // 8, unpack, 0)


def per_device(positions, normals, curvature, pair_targets, pair_sources, pair_count, node_counts, drop_clusters, drop_owner):
    local, _, nodes = positions.shape
    nrow, ncol = lax.axis_size("row"), lax.axis_size("col")
    devs = nrow * ncol
    me = lax.axis_index("row") * ncol + lax.axis_index("col")
    cap = max(2, 2 * local // devs)
    per_drop = drop_clusters.shape[1]
    drops = drop_owner.shape[0]
    here = local // per_drop
    ints = jnp.int32

    flat_clusters = drop_clusters.reshape(-1)
    flat_counts = node_counts.reshape(-1)
    flat_owner = jnp.broadcast_to(drop_owner[:, None], (drops, per_drop)).reshape(-1)
    order = jnp.arange(local, dtype=ints)
    hit = (me * local + order)[:, None] == flat_clusters[None, :]
    home_counts = jnp.sum(jnp.where(hit, flat_counts[None, :], 0), axis=1, dtype=ints)
    home_owner = jnp.sum(jnp.where(hit, flat_owner[None, :], 0), axis=1, dtype=ints)
    rank = jnp.sum((home_owner[None, :] == home_owner[:, None]) & (order[None, :] < order[:, None]), axis=1, dtype=ints)
    slot_of = home_owner * cap + rank
    all_slots = jnp.arange(devs * cap, dtype=ints)
    pack = jnp.sum(jnp.where(slot_of[None, :] == all_slots[:, None], order[None, :], 0), axis=1, dtype=ints)

    drop_ids = jnp.arange(drops, dtype=ints)
    mine = drop_owner == me
    place = jnp.sum(mine[None, :] & (drop_ids[None, :] < drop_ids[:, None]), axis=1, dtype=ints)
    chosen = mine[None, :] & (place[None, :] == jnp.arange(here, dtype=ints)[:, None])
    owned_clusters = jnp.sum(jnp.where(chosen[:, :, None], drop_clusters[None], 0), axis=1, dtype=ints).reshape(-1)
    owned_counts = jnp.sum(jnp.where(chosen[:, :, None], node_counts[None], 0), axis=1, dtype=ints).reshape(-1)
    anchor = owned_clusters // local
    before = (anchor[None, :] == anchor[:, None]) & (owned_clusters[None, :] < owned_clusters[:, None])
    place_in = jnp.sum(before, axis=1, dtype=ints)

    dma = pltpu.SemaphoreType.DMA
    f32 = jnp.float32
    targets, sources = pl.pallas_call(
        functools.partial(gather_kernel, nrow, ncol),
        out_shape=(jax.ShapeDtypeStruct((ncol, 3, local, nodes), f32), jax.ShapeDtypeStruct((nrow, 6, local, nodes), f32)),
        in_specs=[VMEM] * 4, out_specs=(VMEM, VMEM),
        scratch_shapes=[dma((ncol - 1,)), dma((ncol - 1,)), dma((2 * nrow - 2,)), dma((2 * nrow - 2,))],
        compiler_params=pltpu.CompilerParams(collective_id=0, has_side_effects=True, vmem_limit_bytes=56 << 20),
        name="gather_blocks",
    )(positions, normals, curvature, home_counts[:, None])
    speeds = pl.pallas_call(
        pair_kernel,
        out_shape=jax.ShapeDtypeStruct((ncol, 3, local, nodes), f32),
        in_specs=[SMEM] * 3 + [VMEM] * 2, out_specs=VMEM,
        scratch_shapes=[pltpu.VMEM((ncol * local, 8, nodes), f32), pltpu.VMEM((nrow * local, 8, nodes), f32)],
        compiler_params=pltpu.CompilerParams(vmem_limit_bytes=56 << 20),
        name="pairs",
    )(pair_targets, pair_sources, pair_count, targets, sources)
    return pl.pallas_call(
        functools.partial(home_kernel, nrow, ncol, cap),
        out_shape=jax.ShapeDtypeStruct((local, 3, nodes), f32),
        in_specs=[SMEM] * 4 + [VMEM], out_specs=VMEM,
        scratch_shapes=[
            pltpu.VMEM((ncol - 1, 3, local, nodes), f32), pltpu.VMEM((max(ncol // 2 - 1, 1), 3, local, nodes), f32),
            pltpu.VMEM((local, 8, nodes), f32),
            pltpu.VMEM((devs, 3, cap, nodes), f32), pltpu.VMEM((devs, 3, cap, nodes), f32),
            dma((ncol - 1,)), dma((ncol - 1,)), dma((devs - 1,)), dma((devs - 1,)),
        ],
        compiler_params=pltpu.CompilerParams(collective_id=1, has_side_effects=True, vmem_limit_bytes=56 << 20),
        name="to_owners",
    )(pack, anchor, place_in, owned_counts, speeds)


def solution(mesh):
    every = ("groups", "row", "col")
    in_specs = (
        P(every, None, None), P(every, None, None), P(every, None), P(every, None), P(every, None), P(every),
        P("groups", None), P("groups", None), P("groups"),
    )
    return jax.shard_map(per_device, mesh=mesh, in_specs=in_specs, out_specs=P(every, None, None), check_vma=False)
```

```python
import functools
import math

import jax
import jax.numpy as jnp
from jax import lax
from jax.experimental import pallas as pl
from jax.experimental.pallas import tpu as pltpu
from jax.sharding import PartitionSpec as P

regular_sq = 0.0025
stokes_scale = 1.0 / (8.0 * math.pi)
MESH = pl.DeviceIdType.MESH
VMEM = pl.BlockSpec(memory_space=pltpu.VMEM)
SMEM = pl.BlockSpec(memory_space=pltpu.SMEM)


unroll = 32


def gather_kernel(nrow, ncol, pos_ref, nrm_ref, curv_ref, cnt_ref, t_ref, s_ref, tsend, trecv, ssend, srecv):
    row, col = lax.axis_index("row"), lax.axis_index("col")
    barrier = pltpu.get_barrier_semaphore()
    for d in range(1, nrow):
        pl.semaphore_signal(barrier, inc=1, device_id={"row": lax.rem(row + d, nrow)}, device_id_type=MESH)
    for d in range(1, ncol):
        pl.semaphore_signal(barrier, inc=1, device_id={"col": lax.rem(col + d, ncol)}, device_id_type=MESH)
    live = lax.broadcasted_iota(jnp.int32, curv_ref.shape, 1) < cnt_ref[...]
    scale = jnp.where(live, curv_ref[...], 0.0)
    for k in range(3):
        coord = pos_ref[k]
        t_ref[col, k] = coord
        s_ref[row, k] = coord
        s_ref[row, 3 + k] = scale * nrm_ref[k]
    pl.semaphore_wait(barrier, nrow + ncol - 2)
    copies = []
    for d in range(1, ncol):
        copies.append(pltpu.make_async_remote_copy(
            src_ref=t_ref.at[col], dst_ref=t_ref.at[col],
            send_sem=tsend.at[d - 1], recv_sem=trecv.at[d - 1],
            device_id={"col": lax.rem(col + d, ncol)}, device_id_type=MESH))

    def relay(way, step):
        block = jnp.clip(row - way * step, 0, nrow - 1)
        to = jnp.clip(row + way, 0, nrow - 1)
        at = step if way > 0 else nrow - 1 + step
        return pltpu.make_async_remote_copy(
            src_ref=s_ref.at[block], dst_ref=s_ref.at[block],
            send_sem=ssend.at[at], recv_sem=srecv.at[at],
            device_id={"row": to}, device_id_type=MESH)

    def sends(way, step):
        return (row < nrow - 1) & (row >= step) if way > 0 else (row > 0) & (row + step < nrow)

    def receives(way, step):
        return row >= step + 1 if way > 0 else row + step + 1 < nrow

    for step in range(nrow - 1):
        for way in (1, -1):
            if step > 0:
                @pl.when(receives(way, step - 1))
                def _():
                    relay(way, step - 1).wait_recv()

            @pl.when(sends(way, step))
            def _():
                relay(way, step).start()
        if step == 0:
            for copy in copies:
                copy.start()
    for way in (1, -1):
        @pl.when(receives(way, nrow - 2))
        def _():
            relay(way, nrow - 2).wait_recv()
        for step in range(nrow - 1):
            @pl.when(sends(way, step))
            def _():
                relay(way, step).wait_send()
    for copy in copies:
        copy.wait()


def split3(x):
    high = x.astype(jnp.bfloat16).astype(jnp.float32)
    rest = x - high
    middle = rest.astype(jnp.bfloat16).astype(jnp.float32)
    return high, middle, rest - middle


def split2(x):
    high = x.astype(jnp.bfloat16)
    return high, (x - high.astype(jnp.float32)).astype(jnp.bfloat16)


def pair_kernel(tgt_ref, src_ref, count_ref, t_ref, s_ref, v_ref, tc_ref, sc_ref):
    ncol, _, local, _ = t_ref.shape
    nrow = s_ref.shape[0]
    slots = tgt_ref.shape[1]
    f32 = jnp.float32
    v_ref[...] = jnp.zeros_like(v_ref)

    def targets(c, carry):
        rows = pl.ds(pl.multiple_of(c * local, local), local)
        square = jnp.full((local, 128), regular_sq, f32)
        for k in range(3):
            coord = t_ref[c, k]
            centre = jnp.mean(coord, axis=1, keepdims=True)
            coord = coord - centre
            square = square + coord * coord
            tc_ref[rows, k, :] = coord
            tc_ref[rows, 5 + k, :] = jnp.broadcast_to(centre, coord.shape)
        tc_ref[rows, 3, :] = square
        tc_ref[rows, 4, :] = jnp.ones((local, 128), f32)
        return carry

    lax.fori_loop(0, ncol, targets, 0)

    def sources(r, carry):
        rows = pl.ds(pl.multiple_of(r * local, local), local)
        for k in range(6):
            sc_ref[rows, k, :] = s_ref[r, k]
        return carry

    lax.fori_loop(0, nrow, sources, 0)
    count = count_ref[0]
    ones = jnp.ones((1, 128), f32)
    none = jnp.zeros((3, 128), f32)

    def many(block, carry):
        made = []
        for u in range(unroll):
            e = block * unroll + u
            active = e < count
            e = jnp.minimum(e, slots - 1)
            t, s = tgt_ref[0, e], src_ref[0, e]
            near = tc_ref[t]
            far = sc_ref[s]
            shifted = far[0:3] - near[5:8]
            force = jnp.where(active, far[3:6], 0.0)
            square = jnp.sum(shifted * shifted, axis=0, keepdims=True)
            along = jnp.sum(shifted * force, axis=0, keepdims=True)
            a_hi, a_mid, a_lo = split3(jnp.concatenate([near[0:5], none], axis=0))
            b_hi, b_mid, b_lo = split3(jnp.concatenate([-2.0 * shifted, ones, square, none], axis=0))
            c_hi, c_mid, c_lo = split3(jnp.concatenate([force, 0.0 * ones, -along, none], axis=0))
            right = jnp.concatenate([a_hi, a_mid, a_lo, a_hi, a_mid, a_hi], axis=0).astype(jnp.bfloat16)
            left = jnp.concatenate([
                jnp.concatenate([b_hi, b_hi, b_hi, b_mid, b_mid, b_lo], axis=0),
                jnp.concatenate([c_hi, c_hi, c_hi, c_mid, c_mid, c_lo], axis=0)], axis=1).astype(jnp.bfloat16)
            both = lax.dot_general(left, right, (((0,), (0,)), ((), ())), preferred_element_type=f32)
            gathered = jnp.concatenate([force, shifted, ones, ones], axis=0)
            g_hi = gathered.astype(jnp.bfloat16).astype(f32)
            g = jnp.concatenate([g_hi, gathered - g_hi], axis=0).astype(jnp.bfloat16)
            made.append((t, near, both, g))
        results = []
        for t, near, both, g in made:
            inv = lax.rsqrt(both[0:128])
            weight = inv * inv * inv
            iso_hi, iso_lo = split2(inv + regular_sq * weight)
            pro_hi, pro_lo = split2(both[128:256] * weight)
            m = jnp.concatenate([
                jnp.concatenate([iso_hi, pro_hi], axis=1), jnp.concatenate([iso_lo, pro_lo], axis=1)], axis=0)
            out = jnp.dot(jnp.concatenate([g, g], axis=1), m, preferred_element_type=f32)
            out = out[0:8] + out[8:16]
            results.append((t, stokes_scale * (out[0:3, 0:128] + near[0:3] * out[6:7, 128:256] - out[3:6, 128:256])))
        for t, speed in results:
            c, i = t // local, lax.rem(t, local)
            for k in range(3):
                v_ref[c, k, pl.ds(i, 1), :] += speed[k:k + 1]
        return carry

    lax.fori_loop(0, (count + unroll - 1) // unroll, many, 0)


def home_kernel(nrow, ncol, cap, pack_ref, from_ref, rank_ref, cnt_ref, v_ref, out_ref, got, part, home, outg, arr, vsend, vrecv, asend, arecv):
    row, col = lax.axis_index("row"), lax.axis_index("col")
    local = out_ref.shape[1]
    devs = nrow * ncol
    me = row * ncol + col
    barrier = pltpu.get_barrier_semaphore()

    def peer(d):
        p = lax.rem(me + d, devs)
        return {"row": p // ncol, "col": lax.rem(p, ncol)}

    for d in range(1, devs):
        pl.semaphore_signal(barrier, inc=1, device_id=peer(d), device_id_type=MESH)
    pl.semaphore_wait(barrier, devs - 1)
    half = ncol // 2
    core = lax.rem(col, 2)
    mine_x = col // 2
    within, across = [], []
    for d in [*range(1, half), 0]:
        x = lax.rem(mine_x + d, half)
        within.append(pltpu.make_async_remote_copy(
            src_ref=v_ref.at[2 * x + 1 - core], dst_ref=got.at[d], send_sem=vsend.at[d], recv_sem=vrecv.at[d],
            device_id={"col": col + 1 - 2 * core}, device_id_type=MESH))
    for copy in within:
        copy.start()
    for d in range(1, half):
        to = 2 * lax.rem(mine_x + d, half) + core
        within[d - 1].wait_recv()
        part[d - 1] = v_ref[to] + got[d]
        copy = pltpu.make_async_remote_copy(
            src_ref=part.at[d - 1], dst_ref=got.at[half + d - 1],
            send_sem=vsend.at[half + d - 1], recv_sem=vrecv.at[half + d - 1],
            device_id={"col": to}, device_id_type=MESH)
        copy.start()
        across.append(copy)
    within[half - 1].wait_recv()
    for copy in across:
        copy.wait_recv()
    for k in range(3):
        mine = v_ref[col, k] + got[0, k]
        for d in range(1, half):
            mine = mine + got[half + d - 1, k]
        home[:, k, :] = mine
    for copy in within + across:
        copy.wait_send()

    def pack(p, carry):
        for j in range(cap):
            one = home[pack_ref[p * cap + j]]
            for k in range(3):
                outg[p, k, j:j + 1, :] = one[k:k + 1]
        return carry

    lax.fori_loop(0, devs, pack, 0)
    copies = []
    for d in range(1, devs):
        copies.append(pltpu.make_async_remote_copy(
            src_ref=outg.at[lax.rem(me + d, devs)], dst_ref=arr.at[me],
            send_sem=asend.at[d - 1], recv_sem=arecv.at[d - 1],
            device_id=peer(d), device_id_type=MESH))
    for copy in copies:
        copy.start()
    arr[me] = outg[me]
    for copy in copies:
        copy.wait()
    slots = lax.broadcasted_iota(jnp.int32, (1, 128), 1)

    def unpack(i, carry):
        for u in range(8):
            n = i * 8 + u
            at, place = from_ref[n], rank_ref[n]
            live = slots < cnt_ref[n]
            for k in range(3):
                out_ref[k, pl.ds(n, 1), :] = jnp.where(live, arr[at, k, pl.ds(place, 1), :], 0.0)
        return carry

    lax.fori_loop(0, local // 8, unpack, 0)


def per_device(positions, normals, curvature, pair_targets, pair_sources, pair_count, node_counts, drop_clusters, drop_owner):
    local, _, nodes = positions.shape
    nrow, ncol = lax.axis_size("row"), lax.axis_size("col")
    devs = nrow * ncol
    me = lax.axis_index("row") * ncol + lax.axis_index("col")
    cap = max(2, 2 * local // devs)
    per_drop = drop_clusters.shape[1]
    drops = drop_owner.shape[0]
    here = local // per_drop
    ints = jnp.int32

    flat_clusters = drop_clusters.T.reshape(-1)
    flat_counts = node_counts.T.reshape(-1)
    flat_owner = jnp.broadcast_to(drop_owner[None, :], (per_drop, drops)).reshape(-1)
    order = jnp.arange(local, dtype=ints)
    hit = (me * local + order)[:, None] == flat_clusters[None, :]
    home_counts = jnp.sum(jnp.where(hit, flat_counts[None, :], 0), axis=1, dtype=ints)
    home_owner = jnp.sum(jnp.where(hit, flat_owner[None, :], 0), axis=1, dtype=ints)
    rank = jnp.sum((home_owner[None, :] == home_owner[:, None]) & (order[None, :] < order[:, None]), axis=1, dtype=ints)
    slot_of = home_owner * cap + rank
    all_slots = jnp.arange(devs * cap, dtype=ints)
    pack = jnp.sum(jnp.where(slot_of[None, :] == all_slots[:, None], order[None, :], 0), axis=1, dtype=ints)

    drop_ids = jnp.arange(drops, dtype=ints)
    mine = drop_owner == me
    place = jnp.sum(mine[None, :] & (drop_ids[None, :] < drop_ids[:, None]), axis=1, dtype=ints)
    chosen = mine[None, :] & (place[None, :] == jnp.arange(here, dtype=ints)[:, None])
    owned_clusters = jnp.sum(jnp.where(chosen[:, :, None], drop_clusters[None], 0), axis=1, dtype=ints).reshape(-1)
    owned_counts = jnp.sum(jnp.where(chosen[:, :, None], node_counts[None], 0), axis=1, dtype=ints).reshape(-1)
    anchor = owned_clusters // local
    before = (anchor[None, :] == anchor[:, None]) & (owned_clusters[None, :] < owned_clusters[:, None])
    place_in = jnp.sum(before, axis=1, dtype=ints)

    dma = pltpu.SemaphoreType.DMA
    f32 = jnp.float32
    targets, sources = pl.pallas_call(
        functools.partial(gather_kernel, nrow, ncol),
        out_shape=(jax.ShapeDtypeStruct((ncol, 3, local, nodes), f32), jax.ShapeDtypeStruct((nrow, 6, local, nodes), f32)),
        in_specs=[VMEM] * 4, out_specs=(VMEM, VMEM),
        scratch_shapes=[dma((ncol - 1,)), dma((ncol - 1,)), dma((2 * nrow - 2,)), dma((2 * nrow - 2,))],
        compiler_params=pltpu.CompilerParams(collective_id=0, has_side_effects=True, vmem_limit_bytes=56 << 20),
        name="gather_blocks",
    )(jnp.transpose(positions, (1, 0, 2)), jnp.transpose(normals, (1, 0, 2)), curvature, home_counts[:, None])
    speeds = pl.pallas_call(
        pair_kernel,
        out_shape=jax.ShapeDtypeStruct((ncol, 3, local, nodes), f32),
        in_specs=[SMEM] * 3 + [VMEM] * 2, out_specs=VMEM,
        scratch_shapes=[pltpu.VMEM((ncol * local, 8, nodes), f32), pltpu.VMEM((nrow * local, 8, nodes), f32)],
        compiler_params=pltpu.CompilerParams(vmem_limit_bytes=56 << 20),
        name="pairs",
    )(pair_targets, pair_sources, pair_count, targets, sources)
    owned = pl.pallas_call(
        functools.partial(home_kernel, nrow, ncol, cap),
        out_shape=jax.ShapeDtypeStruct((3, local, nodes), f32),
        in_specs=[SMEM] * 4 + [VMEM], out_specs=VMEM,
        scratch_shapes=[
            pltpu.VMEM((ncol - 1, 3, local, nodes), f32), pltpu.VMEM((max(ncol // 2 - 1, 1), 3, local, nodes), f32),
            pltpu.VMEM((local, 8, nodes), f32),
            pltpu.VMEM((devs, 3, cap, nodes), f32), pltpu.VMEM((devs, 3, cap, nodes), f32),
            dma((ncol - 1,)), dma((ncol - 1,)), dma((devs - 1,)), dma((devs - 1,)),
        ],
        compiler_params=pltpu.CompilerParams(collective_id=1, has_side_effects=True, vmem_limit_bytes=56 << 20),
        name="to_owners",
    )(pack, anchor, place_in, owned_counts, speeds)
    return jnp.transpose(owned, (1, 0, 2))


def solution(mesh):
    every = ("groups", "row", "col")
    in_specs = (
        P(every, None, None), P(every, None, None), P(every, None), P(every, None), P(every, None), P(every),
        P("groups", None), P("groups", None), P("groups"),
    )
    return jax.shard_map(per_device, mesh=mesh, in_specs=in_specs, out_specs=P(every, None, None), check_vma=False)
```
